32 devices in a mesh: grp: 2 (over x), tp: 16 (over z, y, core).
Axes of the slice: x: 2, y: 2, z: 4, core: 2. Of those that a mesh axis runs over, the one named last changes fastest.
Arguments:
- tokens: bfloat16 [8192, 256], P('tp', 'grp'), parts along dimension 1, may hold values from -400 to 400
- norm_gain: bfloat16 [8192], P('tp'), may hold values from 0.099609375 to 1.8984375
- gate_weight: bfloat16 [8192, 28672], P(None, 'tp'), may hold values from -0.0625 to 0.0625
- up_weight: bfloat16 [8192, 28672], P(None, 'tp'), may hold values from -0.0625 to 0.0625
- down_weight: bfloat16 [28672, 8192], P('tp'), may hold values from -0.046875 to 0.046875
- target: bfloat16 [8192, 256], P('tp', 'grp'), parts along dimension 1, may hold values from -6 to 6
- probe_seeds: int32 [4], P('grp'), parts along dimension 0, may hold values from 0 to 1073741823
Outputs:
- unit_traces: float32 [6, 28672], P('grp', 'tp'), parts along dimension 0
The draws below stay inside these ranges and needn't reach their ends.
There are 2 independent parts, one for each index of `grp`. The reference program is written for one: setup_inputs(seed, part) draws one part's arguments, and reference() takes and returns one part's arrays. A program takes and returns all parts, laid end to end along the dimension named above; an argument that names none is the same for every part. Nothing has to cross between parts.
All inputs are finite; a program needn't handle non-finite values.
Results may differ from the reference program's by a relative error of at most 0.0029.
Values may be sent and summed in bfloat16 or wider, within the bound.
A program may use at most 256 MiB of HBM per device.

```python
import math
import jax
import jax.numpy as jnp
from jax import lax

D = 8192
FF = 28672
TOK = 128
PROBES = 2


def draw_tokens(key, part):
    key = jax.random.fold_in(key, 11)
    key_feat, key_tok, key_base = jax.random.split(key, 3)
    ramp = 3.0 ** (0.5 * jnp.arange(D, dtype=jnp.float32) / D)
    feature_scale = jnp.exp(jax.random.uniform(key_feat, (D, 1), minval=0.0, maxval=math.log(10.0)))
    token_scale = jnp.exp(jax.random.uniform(key_tok, (1, TOK), minval=0.0, maxval=math.log(10.0)))
    base_values = jnp.clip(jax.random.normal(key_base, (D, TOK)), -5.0, 5.0)
    values = base_values * feature_scale * token_scale * ramp[:, None] * 0.3
    return values.astype(jnp.bfloat16)


def strengthened(result, rng, source, target, shards_of, factor):
    owner, partner = [(jnp.arange(result.shape[dim]) // (result.shape[dim] // shards_of)).reshape([-1 if axis == dim else 1 for axis in range(result.ndim)]) for dim in (source, target)]
    chosen = jax.random.permutation(rng, shards_of)[partner]
    strong = (owner == chosen) | (owner == (partner + shards_of // 2) % shards_of)
    return jnp.where(strong, factor * result, result)


def shard_levels(key, extent, cuts, low, largest):
    level = 1.0
    for position, blocks in cuts:
        steps = jax.random.uniform(jax.random.fold_in(jax.random.fold_in(key, 6), position), (blocks,), jnp.float32, low / len(cuts), largest / len(cuts))
        level = level * jnp.repeat(jnp.exp(steps), extent[position] // blocks).reshape((-1,) + (1,) * (len(extent) - 1 - position))
    return level


def noise(key, extent, scale, most, cuts=(), kind=jnp.bfloat16):
    factor_of = shard_levels(key, extent, cuts, -0.22, 0.18) if cuts else 1.0
    entries = jax.random.normal(key, extent, jnp.float32) * scale * factor_of
    return jnp.minimum(jnp.maximum(entries, -most), most).astype(kind)


def noise_with(own_key, shape, spread, limit, cuts, heavy, held_as=jnp.bfloat16):
    array = spread * jax.random.normal(own_key, shape, jnp.float32)
    if cuts:
        array = array * shard_levels(own_key, shape, cuts, -0.22, 0.18)
    return jnp.clip(strengthened(array, jax.random.fold_in(own_key, 3), *heavy), -limit, limit).astype(held_as)


def setup_inputs(seed: int = 0, part: int = 0) -> dict:
    arg_keys = jax.random.split(jax.random.key(seed), 8)
    own_keys = jax.random.split(jax.random.fold_in(arg_keys[7], part), 8)
    tokens = draw_tokens(jax.random.fold_in(jax.random.fold_in(arg_keys[7], part), 71), part)
    norm_gain = jnp.clip(1.0 + 0.18 * jax.random.normal(arg_keys[1], (D,), jnp.float32), 0.099609375, 1.8984375).astype(jnp.bfloat16)
    gate_weight = noise(arg_keys[2], (D, FF), D ** -0.5, 0.0625, ((1, 16),))
    up_weight = noise(arg_keys[3], (D, FF), D ** -0.5, 0.0625, ((1, 16),))
    down_weight = noise_with(arg_keys[4], (FF, D), FF ** -0.5, 0.046875, ((0, 16),), (0, 1, 16, 2.0))
    target = noise(own_keys[5], (D, TOK), 1.0, 6.0, ((0, 16),))
    probe_seeds = jax.random.randint(own_keys[6], (PROBES,), 0, 1073741824).astype(jnp.int32)
    return {"tokens": tokens, "norm_gain": norm_gain, "gate_weight": gate_weight, "up_weight": up_weight, "down_weight": down_weight, "target": target, "probe_seeds": probe_seeds}


EPSILON = 1e-05
LEADING = (((0,), (0,)), ((), ()))

def mixing(mixed_word):
    mixed_word = mixed_word ^ lax.shift_right_logical(mixed_word, jnp.int32(16))
    mixed_word = mixed_word * jnp.int32(73244475)
    mixed_word = mixed_word ^ lax.shift_right_logical(mixed_word, jnp.int32(15))
    mixed_word = mixed_word * jnp.int32(73244475)
    return mixed_word ^ lax.shift_right_logical(mixed_word, jnp.int32(16))

def sign_table(probe_seed, base, row_offset, col_offset, row_count, col_count, stride):
    row_ids = lax.broadcasted_iota(jnp.int32, (row_count, col_count), 0) + row_offset
    col_ids = lax.broadcasted_iota(jnp.int32, (row_count, col_count), 1) + col_offset
    index_table = (base + row_ids * stride + col_ids).astype(jnp.int32)
    word = mixing(mixing(probe_seed) ^ index_table)
    return (1 - 2 * (word & 1)).astype(jnp.bfloat16)

def lead_product(left, right):
    return lax.dot_general(left, right, LEADING, preferred_element_type=jnp.float32)

def hidden_state(normed, gate_weight, up_weight, probe_seeds, block_start, block_width):
    gate_cols = lax.dynamic_slice_in_dim(gate_weight, block_start, block_width, 1)
    up_cols = lax.dynamic_slice_in_dim(up_weight, block_start, block_width, 1)
    gate_pre = lead_product(gate_cols, normed)
    up_pre = lead_product(up_cols, normed)
    gate_dots = []
    up_dots = []
    for probe_index in range(PROBES):
        probe_seed = probe_seeds[probe_index]
        gate_signs = sign_table(probe_seed, 0, 0, block_start, D, block_width, FF)
        up_signs = sign_table(probe_seed, D * FF, 0, block_start, D, block_width, FF)
        gate_dots.append(lead_product(gate_signs, normed) * D ** (-0.5))
        up_dots.append(lead_product(up_signs, normed) * D ** (-0.5))
    sigmoid_gate = jax.nn.sigmoid(gate_pre)
    activated = gate_pre * sigmoid_gate
    first_d = sigmoid_gate * (1.0 + gate_pre * (1.0 - sigmoid_gate))
    second_d = sigmoid_gate * (1.0 - sigmoid_gate) * (2.0 + gate_pre * (1.0 - 2.0 * sigmoid_gate))
    hidden = (activated * up_pre).astype(jnp.bfloat16)
    hidden_dots = [(first_d * gate_dots[p_index] * up_pre + activated * up_dots[p_index]).astype(jnp.bfloat16) for p_index in range(PROBES)]
    return (gate_pre, up_pre, gate_dots, up_dots, activated, first_d, second_d, hidden, hidden_dots)

def reference(tokens, norm_gain, gate_weight, up_weight, down_weight, target, probe_seeds):
    widened = tokens.astype(jnp.float32)
    mean_square = lax.optimization_barrier(jnp.mean(widened * widened, axis=0))
    normed = (widened * lax.rsqrt(mean_square + EPSILON)[None, :] * norm_gain.astype(jnp.float32)[:, None]).astype(jnp.bfloat16)
    block_width = math.gcd(FF, 1024)
    block_total = FF // block_width
    block_ids = jnp.arange(block_total, dtype=jnp.int32)

    def forward(totals, block_index):
        block_start = block_index * block_width
        state = hidden_state(normed, gate_weight, up_weight, probe_seeds, block_start, block_width)
        hidden = state[7]
        hidden_dots = state[8]
        down_rows = lax.dynamic_slice_in_dim(down_weight, block_start, block_width, 0)
        parts = [lead_product(down_rows, hidden)]
        for probe_index in range(PROBES):
            down_signs = sign_table(probe_seeds[probe_index], 2 * D * FF, block_start, 0, block_width, D, D)
            parts.append(lead_product(down_rows, hidden_dots[probe_index]) + lead_product(down_signs, hidden) * FF ** (-0.5))
        return (totals + jnp.stack(parts), None)
    initial = jnp.zeros((1 + PROBES, D, TOK), jnp.float32)
    totals, _ = lax.scan(forward, initial, block_ids)
    grad_out = ((totals[0] - target.astype(jnp.float32)) / TOK).astype(jnp.bfloat16)
    tangent_outs = totals[1:].astype(jnp.bfloat16)

    def backward(block_index):
        block_start = block_index * block_width
        gate_pre, up_pre, gate_dots, up_dots, activated, first_d, second_d, hidden, hidden_dots = hidden_state(normed, gate_weight, up_weight, probe_seeds, block_start, block_width)
        down_rows = lax.dynamic_slice_in_dim(down_weight, block_start, block_width, 0)
        back = jnp.dot(down_rows, grad_out, preferred_element_type=jnp.float32)
        gate_trace = jnp.zeros((block_width,), jnp.float32)
        up_trace = jnp.zeros((block_width,), jnp.float32)
        down_trace = jnp.zeros((block_width,), jnp.float32)
        for probe_index in range(PROBES):
            down_signs = sign_table(probe_seeds[probe_index], 2 * D * FF, block_start, 0, block_width, D, D)
            cross = jnp.dot(down_rows, tangent_outs[probe_index], preferred_element_type=jnp.float32) / TOK
            probe_grad = jnp.dot(down_signs, grad_out, preferred_element_type=jnp.float32) * FF ** (-0.5)
            probe_tan = jnp.dot(down_signs, tangent_outs[probe_index], preferred_element_type=jnp.float32) * FF ** (-0.5) / TOK
            dd_hidden = cross + probe_grad
            gate_dot = gate_dots[probe_index]
            up_dot = up_dots[probe_index]
            dd_gate = dd_hidden * up_pre * first_d + back * up_dot * first_d + back * up_pre * second_d * gate_dot
            dd_up = dd_hidden * activated + back * first_d * gate_dot
            gate_trace = gate_trace + lax.optimization_barrier(jnp.sum(gate_dot * dd_gate, axis=1))
            up_trace = up_trace + lax.optimization_barrier(jnp.sum(up_dot * dd_up, axis=1))
            down_trace = down_trace + lax.optimization_barrier(jnp.sum(hidden_dots[probe_index].astype(jnp.float32) * probe_grad + hidden.astype(jnp.float32) * probe_tan, axis=1))
        return jnp.stack([gate_trace, up_trace, down_trace]) / PROBES
    pieces = lax.map(backward, block_ids)
    return jnp.transpose(pieces, (1, 0, 2)).reshape(3, FF)
```

```python
import functools
import math

import jax
import jax.numpy as jnp
from jax import lax
from jax.experimental import pallas as pl
from jax.experimental.pallas import tpu as pltpu
from jax.sharding import PartitionSpec as P

EPSILON = 1e-05
MIX = 73244475
VMEM_BYTES = 60 * 1024 * 1024


def wrap32(value):
    value &= 0xFFFFFFFF
    return value - (1 << 32) if value >= 1 << 31 else value


LAST_MIX = wrap32((MIX + (1 << 16)) << 15)


def mixing(word):
    word = word ^ lax.shift_right_logical(word, jnp.int32(16))
    word = word * jnp.int32(MIX)
    word = word ^ lax.shift_right_logical(word, jnp.int32(15))
    word = word * jnp.int32(MIX)
    return word ^ lax.shift_right_logical(word, jnp.int32(16))


def sign_tile(seed, base, row0, col0, rows, cols, row_stride, col_stride):
    sub = lax.broadcasted_iota(jnp.int32, (8, 128), 0)
    lane = lax.broadcasted_iota(jnp.int32, (8, 128), 1)
    groups = []
    for group in range(cols // 128):
        index = (
            base
            + (row0 + sub) * row_stride
            + (col0 + group * 128 + lane) * col_stride
        )
        word = seed ^ index
        word = word ^ lax.shift_right_logical(word, jnp.int32(16))
        pieces = [word * jnp.int32(MIX)]
        bit = 8
        while bit < rows:
            flips = [bit * row_stride]
            if flips[0] >= 1 << 16:
                flips.append(flips[0] >> 16)
            delta = None
            for flip in flips:
                plus, minus = jnp.int32(wrap32(MIX * flip)), jnp.int32(wrap32(-MIX * flip))
                term = jnp.where((word & jnp.int32(flip)) != 0, minus, plus)
                delta = term if delta is None else delta + term
            pieces = pieces + [piece + delta for piece in pieces]
            bit *= 2
        signs = []
        for piece in pieces:
            piece = piece ^ lax.shift_right_logical(piece, jnp.int32(15))
            piece = piece * jnp.int32(LAST_MIX)
            signs.append(jnp.where(piece < 0, jnp.float32(-1.0), jnp.float32(1.0)))
        groups.append(jnp.concatenate(signs, axis=0).astype(jnp.bfloat16))
    return jnp.concatenate(groups, axis=1)


def each_block(width, block, body):
    if block % 128 == 0:
        lax.fori_loop(
            0, width // block, lambda i, c: (body(pl.multiple_of(i * block, block)), c)[1], 0
        )
    else:
        for i in range(width // block):
            body(i * block)


def dotf(left, right):
    return jnp.dot(left, right, preferred_element_type=jnp.float32)


def project_kernel(
    model, hidden_units, block, probes,
    scalars, normed_t, normed, gate, up, gate_t, up_t, dots,
):
    step = pl.program_id(0)
    depth, width = gate.shape
    first = scalars[probes]

    @pl.when(step == 0)
    def _():
        gate_t[...] = jnp.zeros_like(gate_t)
        up_t[...] = jnp.zeros_like(up_t)
        dots[...] = jnp.zeros_like(dots)

    aligned = block % 128 == 0
    if not aligned:
        gate_t[...] += dotf(normed_t[...], gate[...])
        up_t[...] += dotf(normed_t[...], up[...])

    def body(start):
        cols = pl.ds(start, block)
        if aligned:
            gate_t[:, cols] += dotf(normed_t[...], gate[:, cols])
            up_t[:, cols] += dotf(normed_t[...], up[:, cols])
        for probe in range(probes):
            for table in range(2):
                tile = sign_tile(
                    scalars[probe], table * model * hidden_units, first + start,
                    step * depth, block, depth, 1, hidden_units,
                )
                dots[2 * probe + table, cols, :] += dotf(tile, normed[...])

    each_block(width, block, body)


def project(scalars, normed_t, normed, gate_weight, up_weight, block, probes, hidden_units):
    model, width = gate_weight.shape
    tokens = normed.shape[1]
    depth = 512
    whole = lambda *shape: pl.BlockSpec(shape, lambda i: (0,) * len(shape))
    rows = lambda cols: pl.BlockSpec((depth, cols), lambda i: (i, 0))
    return pl.pallas_call(
        functools.partial(project_kernel, model, hidden_units, block, probes),
        grid=(model // depth,),
        in_specs=[
            pl.BlockSpec(memory_space=pltpu.SMEM),
            pl.BlockSpec((tokens, depth), lambda i: (0, i)),
            rows(tokens),
            rows(width),
            rows(width),
        ],
        out_specs=[
            whole(tokens, width),
            whole(tokens, width),
            whole(2 * probes, width, tokens),
        ],
        out_shape=[
            jax.ShapeDtypeStruct((tokens, width), jnp.float32),
            jax.ShapeDtypeStruct((tokens, width), jnp.float32),
            jax.ShapeDtypeStruct((2 * probes, width, tokens), jnp.float32),
        ],
        compiler_params=pltpu.CompilerParams(vmem_limit_bytes=VMEM_BYTES),
        cost_estimate=pl.CostEstimate(
            flops=2 * 6 * model * width * tokens * 4,
            bytes_accessed=4 * model * width,
            transcendentals=0,
        ),
        name="project",
    )(scalars, normed_t, normed, gate_weight, up_weight)


def forward_kernel(
    model, hidden_units, block, probe, count, scalars, hidden_t, dot_t, down, out
):
    step = pl.program_id(0)
    width, depth = down.shape
    first = scalars[count]
    out[...] = jnp.zeros_like(out)

    def body(start):
        cols = pl.ds(start, block)
        tile = sign_tile(
            scalars[probe], 2 * model * hidden_units, first + start, step * depth,
            block, depth, model, 1,
        )
        out[...] += dotf(hidden_t[:, cols], tile)

    each_block(width, block, body)
    out[...] = out[...] * hidden_units ** (-0.5) + dotf(dot_t[...], down[...])


def forward(scalars, hidden_t, dot_t, down_weight, block, probe, count, hidden_units):
    width, model = down_weight.shape
    tokens = hidden_t.shape[0]
    depth = 512
    return pl.pallas_call(
        functools.partial(forward_kernel, model, hidden_units, block, probe, count),
        grid=(model // depth,),
        in_specs=[
            pl.BlockSpec(memory_space=pltpu.SMEM),
            pl.BlockSpec((tokens, width), lambda i: (0, 0)),
            pl.BlockSpec((tokens, width), lambda i: (0, 0)),
            pl.BlockSpec((width, depth), lambda i: (0, i)),
        ],
        out_specs=pl.BlockSpec((tokens, depth), lambda i: (0, i)),
        out_shape=jax.ShapeDtypeStruct((tokens, model), jnp.float32),
        compiler_params=pltpu.CompilerParams(vmem_limit_bytes=VMEM_BYTES),
        cost_estimate=pl.CostEstimate(
            flops=2 * 3 * model * width * tokens * 4,
            bytes_accessed=2 * model * width,
            transcendentals=0,
        ),
        name="forward_tangent",
    )(scalars, hidden_t, dot_t, down_weight)


def backward_kernel(
    model, hidden_units, block, probe, count, skip, scalars, grads, down, plain, signed
):
    step = pl.program_id(0)
    width, depth = down.shape
    first = scalars[count]

    @pl.when(step == 0)
    def _():
        plain[...] = jnp.zeros_like(plain)
        signed[...] = jnp.zeros_like(signed)

    def body(start):
        rows = pl.ds(start, block)
        tile = sign_tile(
            scalars[probe], 2 * model * hidden_units, first + start, step * depth,
            block, depth, model, 1,
        )
        plain[rows, :] += dotf(down[rows, :], grads[:, skip:])
        signed[rows, :] += dotf(tile, grads[...])

    each_block(width, block, body)


def backward(scalars, grads, down_weight, block, probe, count, skip, hidden_units):
    width, model = down_weight.shape
    columns = grads.shape[1]
    depth = 512
    return pl.pallas_call(
        functools.partial(backward_kernel, model, hidden_units, block, probe, count, skip),
        grid=(model // depth,),
        in_specs=[
            pl.BlockSpec(memory_space=pltpu.SMEM),
            pl.BlockSpec((depth, columns), lambda i: (i, 0)),
            pl.BlockSpec((width, depth), lambda i: (0, i)),
        ],
        out_specs=[
            pl.BlockSpec((width, columns - skip), lambda i: (0, 0)),
            pl.BlockSpec((width, columns), lambda i: (0, 0)),
        ],
        out_shape=[
            jax.ShapeDtypeStruct((width, columns - skip), jnp.float32),
            jax.ShapeDtypeStruct((width, columns), jnp.float32),
        ],
        compiler_params=pltpu.CompilerParams(vmem_limit_bytes=VMEM_BYTES),
        cost_estimate=pl.CostEstimate(
            flops=2 * 2 * model * width * columns * 2,
            bytes_accessed=2 * model * width,
            transcendentals=0,
        ),
        name="backward",
    )(scalars, grads, down_weight)


def shards(tokens, norm_gain, gate_weight, up_weight, down_weight, target, probe_seeds):
    model, width = gate_weight.shape
    devices = lax.axis_size("tp")
    hidden_units = width * devices
    first_unit = lax.axis_index("tp") * width
    count = tokens.shape[1]
    probes = probe_seeds.shape[0]
    block = math.gcd(width, 256)
    block = block & -block
    scalars = jnp.concatenate([mixing(probe_seeds), first_unit[None].astype(jnp.int32)])

    gathered = lax.all_gather(tokens, "tp", axis=0, tiled=True)
    gain = lax.all_gather(norm_gain, "tp", axis=0, tiled=True)
    widened = gathered.astype(jnp.float32)
    total_squares = jnp.sum(widened * widened, axis=0)
    inverse_rms = lax.rsqrt(total_squares / model + EPSILON)
    normed = (widened * inverse_rms[None, :] * gain.astype(jnp.float32)[:, None]).astype(
        jnp.bfloat16
    )
    gate_t, up_t, dots = project(
        scalars, normed.T, normed, gate_weight, up_weight, block, probes, hidden_units
    )
    gate_pre, up_pre = gate_t.T, up_t.T
    gate_dots = [dots[2 * probe] * model ** (-0.5) for probe in range(probes)]
    up_dots = [dots[2 * probe + 1] * model ** (-0.5) for probe in range(probes)]
    sigmoid_gate = jax.nn.sigmoid(gate_pre)
    activated = gate_pre * sigmoid_gate
    first_d = sigmoid_gate * (1.0 + gate_pre * (1.0 - sigmoid_gate))
    second_d = sigmoid_gate * (1.0 - sigmoid_gate) * (2.0 + gate_pre * (1.0 - 2.0 * sigmoid_gate))
    hidden = (activated * up_pre).astype(jnp.bfloat16)
    hidden_dots = [
        (first_d * gate_dots[p] * up_pre + activated * up_dots[p]).astype(jnp.bfloat16)
        for p in range(probes)
    ]
    hidden_t = hidden.T

    def scatter(value):
        return lax.psum_scatter(value, "tp", scatter_dimension=1, tiled=True)

    output = scatter(dotf(hidden_t, down_weight))
    tangents = [
        scatter(
            forward(
                scalars, hidden_t, hidden_dots[p].T, down_weight, block, p, probes, hidden_units
            )
        )
        for p in range(probes)
    ]
    grad_out = ((output.T - target.astype(jnp.float32)) / count).astype(jnp.bfloat16)
    grad_all = lax.all_gather(grad_out, "tp", axis=0, tiled=True)
    back = None
    gate_trace = up_trace = down_trace = jnp.zeros((width,), jnp.float32)
    for p in range(probes):
        tangent_all = lax.all_gather(
            tangents[p].T.astype(jnp.bfloat16), "tp", axis=0, tiled=True
        )
        skip = count if p else 0
        plain, signed = backward(
            scalars, jnp.concatenate([grad_all, tangent_all], axis=1), down_weight,
            block, p, probes, skip, hidden_units,
        )
        if p == 0:
            back = plain[:, :count]
        cross = plain[:, plain.shape[1] - count :] / count
        probe_grad = signed[:, :count] * hidden_units ** (-0.5)
        probe_tan = signed[:, count:] * hidden_units ** (-0.5) / count
        dd_hidden = cross + probe_grad
        gate_dot, up_dot = gate_dots[p], up_dots[p]
        dd_gate = (
            dd_hidden * up_pre * first_d
            + back * up_dot * first_d
            + back * up_pre * second_d * gate_dot
        )
        dd_up = dd_hidden * activated + back * first_d * gate_dot
        gate_trace = gate_trace + jnp.sum(gate_dot * dd_gate, axis=1)
        up_trace = up_trace + jnp.sum(up_dot * dd_up, axis=1)
        down_trace = down_trace + jnp.sum(
            hidden_dots[p].astype(jnp.float32) * probe_grad
            + hidden.astype(jnp.float32) * probe_tan,
            axis=1,
        )
    return jnp.stack([gate_trace, up_trace, down_trace]) / probes


def solution(mesh):
    return jax.shard_map(
        shards,
        mesh=mesh,
        in_specs=(
            P("tp", "grp"),
            P("tp"),
            P(None, "tp"),
            P(None, "tp"),
            P("tp", None),
            P("tp", "grp"),
            P("grp"),
        ),
        out_specs=P("grp", "tp"),
        check_vma=False,
    )
```

```python
import functools
import math

import jax
import jax.numpy as jnp
from jax import lax
from jax.experimental import pallas as pl
from jax.experimental.pallas import tpu as pltpu
from jax.sharding import PartitionSpec as P

EPSILON = 1e-05
MIX = 73244475
VMEM_BYTES = 60 * 1024 * 1024


def wrap32(value):
    value &= 0xFFFFFFFF
    return value - (1 << 32) if value >= 1 << 31 else value


LAST_MIX = wrap32((MIX + (1 << 16)) << 15)


def mixing(word):
    word = word ^ lax.shift_right_logical(word, jnp.int32(16))
    word = word * jnp.int32(MIX)
    word = word ^ lax.shift_right_logical(word, jnp.int32(15))
    word = word * jnp.int32(MIX)
    return word ^ lax.shift_right_logical(word, jnp.int32(16))


def sign_tile(seed, base, row0, col0, rows, cols, row_stride, col_stride):
    sub = lax.broadcasted_iota(jnp.int32, (8, 128), 0)
    lane = lax.broadcasted_iota(jnp.int32, (8, 128), 1)
    groups = []
    for group in range(cols // 128):
        index = (
            base
            + (row0 + sub) * row_stride
            + (col0 + group * 128 + lane) * col_stride
        )
        word = seed ^ index
        word = word ^ lax.shift_right_logical(word, jnp.int32(16))
        pieces = [word * jnp.int32(MIX)]
        bit = 8
        while bit < rows:
            flips = [bit * row_stride]
            if flips[0] >= 1 << 16:
                flips.append(flips[0] >> 16)
            delta = None
            for flip in flips:
                plus, minus = jnp.int32(wrap32(MIX * flip)), jnp.int32(wrap32(-MIX * flip))
                term = jnp.where((word & jnp.int32(flip)) != 0, minus, plus)
                delta = term if delta is None else delta + term
            pieces = pieces + [piece + delta for piece in pieces]
            bit *= 2
        signs = []
        for piece in pieces:
            piece = piece ^ lax.shift_right_logical(piece, jnp.int32(15))
            piece = piece * jnp.int32(LAST_MIX)
            signs.append(jnp.where(piece < 0, jnp.float32(-1.0), jnp.float32(1.0)))
        groups.append(jnp.concatenate(signs, axis=0).astype(jnp.bfloat16))
    return jnp.concatenate(groups, axis=1)


def each_block(width, block, body):
    if block % 128 == 0:
        lax.fori_loop(
            0, width // block, lambda i, c: (body(pl.multiple_of(i * block, block)), c)[1], 0
        )
    else:
        for i in range(width // block):
            body(i * block)


def dotf(left, right):
    return jnp.dot(left, right, preferred_element_type=jnp.float32)


def project_kernel(
    model, hidden_units, block, probes,
    scalars, normed_t, normed, gate, up, gate_t, up_t, dots,
):
    step = pl.program_id(0)
    depth, width = gate.shape
    first = scalars[probes]

    @pl.when(step == 0)
    def _():
        gate_t[...] = jnp.zeros_like(gate_t)
        up_t[...] = jnp.zeros_like(up_t)
        dots[...] = jnp.zeros_like(dots)

    aligned = block % 128 == 0
    if not aligned:
        gate_t[...] += dotf(normed_t[...], gate[...])
        up_t[...] += dotf(normed_t[...], up[...])

    def body(start):
        cols = pl.ds(start, block)
        if aligned:
            gate_t[:, cols] += dotf(normed_t[...], gate[:, cols])
            up_t[:, cols] += dotf(normed_t[...], up[:, cols])
        for probe in range(probes):
            for table in range(2):
                tile = sign_tile(
                    scalars[probe], table * model * hidden_units, first + start,
                    step * depth, block, depth, 1, hidden_units,
                )
                dots[2 * probe + table, cols, :] += dotf(tile, normed[...])

    each_block(width, block, body)


def project(scalars, normed_t, normed, gate_weight, up_weight, block, probes, hidden_units):
    model, width = gate_weight.shape
    tokens = normed.shape[1]
    depth = 512
    whole = lambda *shape: pl.BlockSpec(shape, lambda i: (0,) * len(shape))
    rows = lambda cols: pl.BlockSpec((depth, cols), lambda i: (i, 0))
    return pl.pallas_call(
        functools.partial(project_kernel, model, hidden_units, block, probes),
        grid=(model // depth,),
        in_specs=[
            pl.BlockSpec(memory_space=pltpu.SMEM),
            pl.BlockSpec((tokens, depth), lambda i: (0, i)),
            rows(tokens),
            rows(width),
            rows(width),
        ],
        out_specs=[
            whole(tokens, width),
            whole(tokens, width),
            whole(2 * probes, width, tokens),
        ],
        out_shape=[
            jax.ShapeDtypeStruct((tokens, width), jnp.float32),
            jax.ShapeDtypeStruct((tokens, width), jnp.float32),
            jax.ShapeDtypeStruct((2 * probes, width, tokens), jnp.float32),
        ],
        compiler_params=pltpu.CompilerParams(vmem_limit_bytes=VMEM_BYTES),
        cost_estimate=pl.CostEstimate(
            flops=2 * 6 * model * width * tokens * 4,
            bytes_accessed=4 * model * width,
            transcendentals=0,
        ),
        name="project",
    )(scalars, normed_t, normed, gate_weight, up_weight)


def forward_kernel(
    model, hidden_units, block, probe, count, scalars, hidden_t, dot_t, down, out
):
    step = pl.program_id(0)
    width, depth = down.shape
    first = scalars[count]
    out[...] = jnp.zeros_like(out)

    def body(start):
        cols = pl.ds(start, block)
        tile = sign_tile(
            scalars[probe], 2 * model * hidden_units, first + start, step * depth,
            block, depth, model, 1,
        )
        out[...] += dotf(hidden_t[:, cols], tile)[None]

    each_block(width, block, body)
    out[...] = out[...] * hidden_units ** (-0.5) + dotf(dot_t[...], down[...])[None]


def forward(scalars, hidden_t, dot_t, down_weight, block, probe, count, hidden_units):
    width, model = down_weight.shape
    tokens = hidden_t.shape[0]
    depth = 512
    return pl.pallas_call(
        functools.partial(forward_kernel, model, hidden_units, block, probe, count),
        grid=(model // depth,),
        in_specs=[
            pl.BlockSpec(memory_space=pltpu.SMEM),
            pl.BlockSpec((tokens, width), lambda i: (0, 0)),
            pl.BlockSpec((tokens, width), lambda i: (0, 0)),
            pl.BlockSpec((width, depth), lambda i: (0, i)),
        ],
        out_specs=pl.BlockSpec((1, tokens, depth), lambda i: (i, 0, 0)),
        out_shape=jax.ShapeDtypeStruct((model // depth, tokens, depth), jnp.float32),
        compiler_params=pltpu.CompilerParams(vmem_limit_bytes=VMEM_BYTES),
        cost_estimate=pl.CostEstimate(
            flops=2 * 3 * model * width * tokens * 4,
            bytes_accessed=2 * model * width,
            transcendentals=0,
        ),
        name="forward_tangent",
    )(scalars, hidden_t, dot_t, down_weight)


def backward_kernel(
    model, hidden_units, block, probe, count, skip, scalars, grad, tangent, down, plain, signed
):
    step = pl.program_id(0)
    width, depth = down.shape
    first = scalars[count]
    grads = jnp.concatenate([grad[...], tangent[...]], axis=1)

    @pl.when(step == 0)
    def _():
        plain[...] = jnp.zeros_like(plain)
        signed[...] = jnp.zeros_like(signed)

    def body(start):
        rows = pl.ds(start, block)
        tile = sign_tile(
            scalars[probe], 2 * model * hidden_units, first + start, step * depth,
            block, depth, model, 1,
        )
        plain[rows, :] += dotf(down[rows, :], grads[:, skip:])
        signed[rows, :] += dotf(tile, grads)

    each_block(width, block, body)


def backward(scalars, grad, tangent, down_weight, block, probe, count, skip, hidden_units):
    width, model = down_weight.shape
    columns = 2 * grad.shape[1]
    depth = 512
    return pl.pallas_call(
        functools.partial(backward_kernel, model, hidden_units, block, probe, count, skip),
        grid=(model // depth,),
        in_specs=[
            pl.BlockSpec(memory_space=pltpu.SMEM),
            pl.BlockSpec((depth, columns // 2), lambda i: (i, 0)),
            pl.BlockSpec((depth, columns // 2), lambda i: (i, 0)),
            pl.BlockSpec((width, depth), lambda i: (0, i)),
        ],
        out_specs=[
            pl.BlockSpec((width, columns - skip), lambda i: (0, 0)),
            pl.BlockSpec((width, columns), lambda i: (0, 0)),
        ],
        out_shape=[
            jax.ShapeDtypeStruct((width, columns - skip), jnp.float32),
            jax.ShapeDtypeStruct((width, columns), jnp.float32),
        ],
        compiler_params=pltpu.CompilerParams(vmem_limit_bytes=VMEM_BYTES),
        cost_estimate=pl.CostEstimate(
            flops=2 * 2 * model * width * columns * 2,
            bytes_accessed=2 * model * width,
            transcendentals=0,
        ),
        name="backward",
    )(scalars, grad, tangent, down_weight)


def shards(tokens, norm_gain, gate_weight, up_weight, down_weight, target, probe_seeds):
    model, width = gate_weight.shape
    devices = lax.axis_size("tp")
    hidden_units = width * devices
    first_unit = lax.axis_index("tp") * width
    count = tokens.shape[1]
    probes = probe_seeds.shape[0]
    block = math.gcd(width, 256)
    block = block & -block
    scalars = jnp.concatenate([mixing(probe_seeds), first_unit[None].astype(jnp.int32)])

    features = tokens.shape[0]
    gain_rows = -(-features // count)
    padded = jnp.pad(norm_gain, (0, gain_rows * count - features)).reshape(gain_rows, count)
    joined = lax.all_gather(jnp.concatenate([tokens, padded], axis=0), "tp", axis=0)
    gathered = joined[:, :features].reshape(model, count)
    gain = joined[:, features:].reshape(devices, gain_rows * count)[:, :features].reshape(model)
    widened = gathered.astype(jnp.float32)
    total_squares = jnp.sum(widened * widened, axis=0)
    inverse_rms = lax.rsqrt(total_squares / model + EPSILON)
    normed = (widened * inverse_rms[None, :] * gain.astype(jnp.float32)[:, None]).astype(
        jnp.bfloat16
    )
    gate_t, up_t, dots = project(
        scalars, normed.T, normed, gate_weight, up_weight, block, probes, hidden_units
    )
    gate_pre, up_pre = gate_t.T, up_t.T
    gate_dots = [dots[2 * probe] * model ** (-0.5) for probe in range(probes)]
    up_dots = [dots[2 * probe + 1] * model ** (-0.5) for probe in range(probes)]
    sigmoid_gate = jax.nn.sigmoid(gate_pre)
    activated = gate_pre * sigmoid_gate
    first_d = sigmoid_gate * (1.0 + gate_pre * (1.0 - sigmoid_gate))
    second_d = sigmoid_gate * (1.0 - sigmoid_gate) * (2.0 + gate_pre * (1.0 - 2.0 * sigmoid_gate))
    hidden = (activated * up_pre).astype(jnp.bfloat16)
    hidden_dots = [
        (first_d * gate_dots[p] * up_pre + activated * up_dots[p]).astype(jnp.bfloat16)
        for p in range(probes)
    ]
    hidden_t = hidden.T

    chips = devices // 2
    core = lax.axis_index("tp") % 2
    swap = [(i, i ^ 1) for i in range(devices)]
    across = [[2 * i + c for i in range(chips)] for c in range(2)]

    def scatter(value):
        if value.shape[0] == devices:
            pairs = value.reshape(chips, 2, count, features)
        else:
            wide = jnp.transpose(value, (1, 0, 2)).reshape(count, chips, 2, features)
            pairs = jnp.transpose(wide, (1, 2, 0, 3))
        mine = lax.dynamic_index_in_dim(pairs, core, 1, keepdims=False)
        other = lax.dynamic_index_in_dim(pairs, 1 - core, 1, keepdims=False)
        sent = (mine + lax.ppermute(other, "tp", swap)).astype(jnp.bfloat16)
        arrived = lax.all_to_all(sent, "tp", 0, 0, axis_index_groups=across, tiled=True)
        return jnp.sum(arrived.astype(jnp.float32), axis=0).T

    primal = dotf(hidden_t, down_weight)
    primal, hidden_t, first_dot = lax.optimization_barrier(
        (primal, hidden_t, hidden_dots[0].T)
    )
    output = lax.psum_scatter(primal, "tp", scatter_dimension=1, tiled=True)
    tangents = []
    dot_t = first_dot
    for p in range(probes):
        tangent = scatter(
            forward(scalars, hidden_t, dot_t, down_weight, block, p, probes, hidden_units)
        ).astype(jnp.bfloat16)
        if p + 1 < probes:
            tangent, dot_t, hidden_t = lax.optimization_barrier(
                (tangent, hidden_dots[p + 1].T, hidden_t)
            )
        tangents.append(tangent)
    grad_out = ((output.T - target.astype(jnp.float32)) / count).astype(jnp.bfloat16)
    grad_all = lax.all_gather(grad_out, "tp", axis=0, tiled=True)
    tangents_all = [lax.all_gather(t, "tp", axis=0, tiled=True) for t in tangents[:-1]]
    tangents_all[0], tangents[-1] = lax.optimization_barrier((tangents_all[0], tangents[-1]))
    tangents_all.append(lax.all_gather(tangents[-1], "tp", axis=0, tiled=True))
    back = None
    gate_trace = up_trace = down_trace = jnp.zeros((width,), jnp.float32)
    for p in range(probes):
        skip = count if p else 0
        plain, signed = backward(
            scalars, grad_all, tangents_all[p], down_weight,
            block, p, probes, skip, hidden_units,
        )
        if p == 0:
            back = plain[:, :count]
        cross = plain[:, plain.shape[1] - count :] / count
        probe_grad = signed[:, :count] * hidden_units ** (-0.5)
        probe_tan = signed[:, count:] * hidden_units ** (-0.5) / count
        dd_hidden = cross + probe_grad
        gate_dot, up_dot = gate_dots[p], up_dots[p]
        dd_gate = (
            dd_hidden * up_pre * first_d
            + back * up_dot * first_d
            + back * up_pre * second_d * gate_dot
        )
        dd_up = dd_hidden * activated + back * first_d * gate_dot
        gate_trace = gate_trace + jnp.sum(gate_dot * dd_gate, axis=1)
        up_trace = up_trace + jnp.sum(up_dot * dd_up, axis=1)
        down_trace = down_trace + jnp.sum(
            hidden_dots[p].astype(jnp.float32) * probe_grad
            + hidden.astype(jnp.float32) * probe_tan,
            axis=1,
        )
    return jnp.stack([gate_trace, up_trace, down_trace]) / probes


def solution(mesh):
    return jax.shard_map(
        shards,
        mesh=mesh,
        in_specs=(
            P("tp", "grp"),
            P("tp"),
            P(None, "tp"),
            P(None, "tp"),
            P("tp", None),
            P("tp", "grp"),
            P("grp"),
        ),
        out_specs=P("grp", "tp"),
        check_vma=False,
    )
```
